512 devices in a mesh: ia: 16 (over z, core), ja: 16 (over y, x_hi), ka: 2 (over x_lo).
Axes of the slice: x: 4 (x_hi: 2, x_lo: 2; x = x_hi * 2 + x_lo), y: 8, z: 8, core: 2. Of those that a mesh axis runs over, the one named last changes fastest.
Arguments:
- tensor: float32 [32, 4096, 4096], P('ka', 'ja', 'ia'), may hold values from -6 to 6
- factor_a: float32 [64, 4096], P('ka', 'ia'), may hold values from -4 to 4
- factor_b: float32 [64, 4096], P('ia', 'ja'), as said below
- factor_c: float32 [64, 32], P('ia', 'ka'), as said below
Outputs:
- gradient: float32 [64, 4096], P('ka', 'ia')
The draws below stay inside these ranges and needn't reach their ends.
Inputs may be any that keep to these rules, and one draw needn't show every extreme that they name: `factor_b`: nonnegative entries. `factor_c`: nonnegative entries.
All inputs are finite; a program needn't handle non-finite values.
Results may differ from the reference program's by a relative error of at most 0.0001.
Values sent between devices are 32-bit elements; how exact they have to be, the bound alone decides.
No kernel may reach another device: no remote copies, remote signals or barrier semaphores. Data moves between devices by JAX's collectives and lax.ppermute only.
A program may use at most 64 MiB of HBM per device.

```python
import jax
import jax.numpy as jnp
from jax import lax

R = 64
I = 4096
J = 4096
K = 32


def draw_factor_b(key, part):
    key = jax.random.fold_in(key, 11)
    first = jax.random.fold_in(key, 0)
    values = jax.random.uniform(first, (R, J), jnp.float32) * (3.0 / J) ** 0.5
    return values


def draw_factor_c(key, part):
    key = jax.random.fold_in(key, 23)
    first = jax.random.fold_in(key, 0)
    values = jax.random.uniform(first, (R, K), jnp.float32) * (3.0 / K) ** 0.5
    return values


def block_scale(key, dims, cuts, low, high):
    def one(axis_at, blocks):
        draws = jax.random.uniform(jax.random.fold_in(jax.random.fold_in(key, 6), axis_at), (blocks,), jnp.float32, low / len(cuts), high / len(cuts))
        return jnp.repeat(jnp.exp(draws), dims[axis_at] // blocks).reshape((-1,) + (1,) * (len(dims) - axis_at - 1))

    factor_of = one(*cuts[0])
    for cut in cuts[1:]:
        factor_of = factor_of * one(*cut)
    return factor_of


def bell_draw(key, extent, spread, limit, pieces=(), held_as=jnp.bfloat16):
    gain = block_scale(key, extent, pieces, -0.22, 0.18) if pieces else 1.0
    array = jax.random.normal(key, extent, jnp.float32) * spread * gain
    return jnp.minimum(jnp.maximum(array, -limit), limit).astype(held_as)


def setup_inputs(seed: int = 0) -> dict:
    splits = jax.random.split(jax.random.key(seed), 5)
    return {
        "tensor": bell_draw(splits[0], (K, J, I), 1.0, 6.0, ((0, 2), (1, 16), (2, 16)), jnp.float32),
        "factor_a": bell_draw(splits[1], (R, I), 0.25, 4.0, ((0, 2), (1, 16)), jnp.float32),
        "factor_b": draw_factor_b(jax.random.fold_in(splits[4], 71), 0),
        "factor_c": draw_factor_c(jax.random.fold_in(splits[4], 71), 0),
    }


def reference(tensor, factor_a, factor_b, factor_c):
    highest = lax.Precision.HIGHEST

    def plane_step(total, items):
        plane_slab, column = items
        term = jnp.dot(factor_b, plane_slab, preferred_element_type=jnp.float32, precision=highest)
        return total + term * column[:, None], None

    start_total = jnp.zeros((factor_a.shape[0], tensor.shape[2]), jnp.float32)
    product, unused = lax.scan(plane_step, start_total, (tensor, factor_c.T))
    gram_b = jnp.dot(factor_b, factor_b.T, preferred_element_type=jnp.float32, precision=highest)
    gram_c = jnp.dot(factor_c, factor_c.T, preferred_element_type=jnp.float32, precision=highest)
    hadamard = gram_b * gram_c
    return product - jnp.dot(hadamard, factor_a, preferred_element_type=jnp.float32, precision=highest)
```

```python
import jax
import jax.numpy as jnp
from jax import lax
from jax.sharding import Mesh, PartitionSpec as P


def local(tensor, factor_a, factor_b, factor_c):
    highest = lax.Precision.HIGHEST
    planes, rows_j, cols = tensor.shape
    share = factor_b.shape[0]
    half = rows_j // 2
    ka = lax.axis_index("ka")
    halves = lax.dynamic_slice_in_dim(factor_b, ka * half, half, 1).reshape(share * half)
    piece = jnp.concatenate([halves, factor_c.reshape(share * planes)])
    peers = lax.axis_size("z") * lax.axis_size("c") * 2
    size = -(-piece.shape[0] // 128) * 128
    piece = jnp.pad(piece, (0, size - piece.shape[0]))
    got = lax.all_to_all(
        jnp.broadcast_to(piece[None, None], (peers, 1, size)), ("z", "c", "ka"), 0, 0, tiled=True
    )
    got = got.reshape(peers // 2, 2, size)
    ranks = peers // 2 * share
    rank_b = got[:, :, : share * half].reshape(peers // 2, 2, share, half)
    rank_b = rank_b.transpose(0, 2, 1, 3).reshape(ranks, rows_j)
    rank_c = got[:, :, share * half : share * (half + planes)].reshape(peers // 2, 2, share, planes)
    all_c = rank_c.transpose(0, 2, 1, 3).reshape(ranks, 2 * planes)
    own_c = lax.dynamic_slice_in_dim(all_c, ka * planes, planes, 1)
    weight = (own_c[:, :, None] * rank_b[:, None, :]).reshape(ranks, planes * rows_j)
    partial = jnp.dot(
        weight,
        tensor.reshape(planes * rows_j, cols),
        preferred_element_type=jnp.float32,
        precision=lax.Precision.HIGH,
    )
    gram_b = jnp.dot(rank_b, rank_b.T, preferred_element_type=jnp.float32, precision=highest)
    gram_c = jnp.dot(all_c, all_c.T, preferred_element_type=jnp.float32, precision=highest)
    share_a = factor_a.shape[0]
    hadamard = lax.dynamic_slice_in_dim(gram_b * gram_c, ka * share_a, share_a, 1)
    partial = partial - jnp.dot(
        hadamard, factor_a, preferred_element_type=jnp.float32, precision=highest
    )
    mine = jnp.tile(partial.reshape(2, share_a, cols), (2, 1, 1))
    x_parts = lax.all_to_all(mine, ("xh", "ka"), 0, 0, tiled=True)
    x_sum = x_parts[0] + x_parts[1] + x_parts[2] + x_parts[3]
    wide = lax.axis_size("y")
    y_parts = lax.all_to_all(
        jnp.broadcast_to(x_sum[None], (wide, share_a, cols)), "y", 0, 0, tiled=True
    )
    return jnp.sum(y_parts, 0)


def solution(mesh):
    sizes = mesh.devices.shape
    fine = Mesh(
        mesh.devices.reshape(sizes[0] // 2, 2, sizes[1] // 2, 2, sizes[2]), ("z", "c", "y", "xh", "ka")
    )
    ia, ja = ("z", "c"), ("y", "xh")
    in_specs = (P("ka", ja, ia), P("ka", ia), P(ia, ja), P(ia, "ka"))
    return jax.shard_map(
        local, mesh=fine, in_specs=in_specs, out_specs=P("ka", ia), check_vma=False
    )
```

```python
import functools

import jax
import jax.numpy as jnp
from jax import lax
from jax.experimental import pallas as pl
from jax.experimental.pallas import tpu as pltpu
from jax.sharding import Mesh, PartitionSpec as P

ORDER = [13, 0, 1, 2, 3, 4, 5, 6, 7, 8, 9, 10, 11, 12, 14, 15]
XAX, YAX = ("y0", "xh", "ka"), ("y2", "y1")
XORD = [3, 0, 1, 2, 4, 5, 6, 7]
YORD = [2, 0, 1, 3]
EARLY, GROUP = 13, 3
VMEM, HBM = pl.BlockSpec(memory_space=pltpu.VMEM), pl.BlockSpec(memory_space=pltpu.HBM)
HIGHEST = lax.Precision.HIGHEST
BF16, F32 = jnp.bfloat16, jnp.float32


def in_hbm(array):
    return pltpu.with_memory_space_constraint(array, pltpu.HBM)


def dot(x, y, precision=None):
    return jnp.dot(x, y, preferred_element_type=F32, precision=precision)


def halves_of(value):
    high = value.astype(BF16)
    return high, (value - high.astype(F32)).astype(BF16)


def message_kernel(b_ref, c_ref, out_ref):
    peers, _, size = out_ref.shape
    share, rows_j = b_ref.shape
    planes = c_ref.shape[1]
    parts = [b_ref[r : r + 1, :] for r in range(share)]
    parts += [c_ref[r : r + 1, :] for r in range(share)]
    pad = size - share * (rows_j + planes)
    if pad:
        parts.append(jnp.zeros((1, pad), F32))
    line = jnp.concatenate(parts, axis=1)
    out_ref[...] = jnp.broadcast_to(line[None], (peers, 1, size))


def split_kernel(t_ref, hi_ref, lo_ref, stage, sems):
    planes, rows_j, _ = stage.shape
    copies = [pltpu.make_async_copy(t_ref.at[k], stage.at[k], sems.at[k]) for k in range(planes)]
    for copy in copies:
        copy.start()
    for k, copy in enumerate(copies):
        copy.wait()
        rows = pl.ds(k * rows_j, rows_j)
        hi_ref[rows, :], lo_ref[rows, :] = halves_of(stage[k])


def product_kernel(got_ref, t_ref, own_ref, other_ref, *refs, share, early):
    if early:
        hi_ref, lo_ref, *refs = refs
    out_ref, b_ref, c_ref, w_ref, acc_ref, stage, sems = refs
    rows_j, cols = b_ref.shape[1], t_ref.shape[2]
    planes = t_ref.shape[0]
    ranks = b_ref.shape[0]

    def copy_of(k):
        return pltpu.make_async_copy(t_ref.at[early + k], stage.at[k], sems.at[k])

    for k in range(planes - early):
        copy_of(k).start()

    @pl.when(lax.axis_index("ka") < 2)
    def _():
        for place, ia in enumerate(ORDER):
            line = got_ref[place, 0:1, :]
            for r in range(share):
                row = ia * share + r
                b_ref[row : row + 1, :] = line[:, r * rows_j : (r + 1) * rows_j]
                first = share * rows_j + r * planes
                c_ref[row : row + 1, :] = line[:, first : first + planes]
        b, c = b_ref[...], c_ref[...]
        gram = dot(b, b.T, HIGHEST) * dot(c, c.T, HIGHEST)
        first_a = lax.axis_index("ka") == 0
        own, other = own_ref[...], other_ref[...]
        all_a = jnp.concatenate([jnp.where(first_a, own, other), jnp.where(first_a, other, own)])
        low = -dot(gram, all_a, HIGHEST)
        total = jnp.zeros((2 * ranks, cols), F32)
        for k in range(planes):
            w_hi, w_lo = halves_of(b * c[:, k : k + 1])
            both = jnp.concatenate([w_hi, w_lo])
            if k < early:
                rows = pl.ds(k * rows_j, rows_j)
                total += dot(both, hi_ref[rows, :])
                low += dot(w_hi, lo_ref[rows, :])
            else:
                w_ref[:, pl.ds((k - early) * rows_j, rows_j)] = both
        acc_ref[...] = total[:ranks] + total[ranks:] + low

    def step(g, carry):
        for k in range(GROUP):
            copy_of(g * GROUP + k).wait()
        total = jnp.zeros((2 * ranks, cols), F32)
        low = acc_ref[...]
        for k in range(GROUP):
            at = g * GROUP + k
            t_hi, t_lo = halves_of(stage[at])
            both = w_ref[:, pl.ds(pl.multiple_of(at * rows_j, rows_j), rows_j)]
            total += dot(both, t_hi)
            low += dot(both[:ranks], t_lo)
        acc_ref[...] = total[:ranks] + total[ranks:] + low
        return carry

    lax.fori_loop(0, (planes - early) // GROUP, step, 0)
    half = own_ref.shape[0]
    for m in range(out_ref.shape[0]):
        out_ref[m] = acc_ref[pl.ds((XORD[m] % 2) * half, half), :]


def size_of(axes):
    size = 1
    for axis in axes:
        size *= lax.axis_size(axis)
    return size


def local(tensor, factor_a, factor_b, factor_c):
    planes, rows_j, cols = tensor.shape
    share = factor_b.shape[0]
    half = factor_a.shape[0]
    peers = lax.axis_size("ia")
    ranks = peers * share
    size = -(-share * (rows_j + planes) // 128) * 128
    message = pl.pallas_call(
        message_kernel,
        out_shape=jax.ShapeDtypeStruct((peers, 1, size), F32),
        in_specs=[VMEM, VMEM],
        out_specs=VMEM,
        compiler_params=pltpu.CompilerParams(vmem_limit_bytes=2**20),
    )(in_hbm(factor_b), in_hbm(factor_c))
    got = lax.all_to_all(message, "ia", 0, 0, tiled=True, axis_index_groups=[ORDER])
    other = lax.ppermute(factor_a, "ka", [(0, 1), (1, 0)])
    tensor = in_hbm(tensor)
    early = []
    if EARLY:
        depth = EARLY * rows_j
        early = pl.pallas_call(
            split_kernel,
            out_shape=[pltpu.VMEM((depth, cols), BF16)] * 2,
            in_specs=[HBM],
            out_specs=[VMEM, VMEM],
            scratch_shapes=[pltpu.VMEM((EARLY, rows_j, cols), F32), pltpu.SemaphoreType.DMA((EARLY,))],
            cost_estimate=pl.CostEstimate(
                flops=4 * depth * cols, bytes_accessed=8 * depth * cols, transcendentals=0
            ),
            compiler_params=pltpu.CompilerParams(vmem_limit_bytes=8 * 2**20),
        )(tensor)
    late = planes - EARLY
    wide_x = size_of(XAX)
    mine = pl.pallas_call(
        functools.partial(product_kernel, share=share, early=EARLY),
        out_shape=jax.ShapeDtypeStruct((wide_x, half, cols), F32),
        in_specs=[VMEM, HBM, VMEM, VMEM] + [VMEM] * len(early),
        out_specs=VMEM,
        scratch_shapes=[
            pltpu.VMEM((ranks, rows_j), F32),
            pltpu.VMEM((ranks, planes), F32),
            pltpu.VMEM((2 * ranks, late * rows_j), BF16),
            pltpu.VMEM((ranks, cols), F32),
            pltpu.VMEM((late, rows_j, cols), F32),
            pltpu.SemaphoreType.DMA((late,)),
        ],
        cost_estimate=pl.CostEstimate(
            flops=6 * ranks * planes * rows_j * cols,
            bytes_accessed=4 * planes * rows_j * cols,
            transcendentals=0,
        ),
        compiler_params=pltpu.CompilerParams(vmem_limit_bytes=12 * 2**20),
    )(got, tensor, factor_a, other, *early)
    x_sum = jnp.sum(lax.all_to_all(mine, XAX, 0, 0, tiled=True, axis_index_groups=[XORD]), 0)
    wide_y = size_of(YAX)
    y_parts = lax.all_to_all(
        jnp.broadcast_to(x_sum[None], (wide_y, half, cols)), YAX, 0, 0, tiled=True, axis_index_groups=[YORD]
    )
    return jnp.sum(y_parts, 0)


def solution(mesh):
    sizes = mesh.devices.shape
    fine = Mesh(
        mesh.devices.reshape(sizes[0], sizes[1] // 8, 2, 2, 2, sizes[2]),
        ("ia", "y2", "y1", "y0", "xh", "ka"),
    )
    ja = ("y2", "y1", "y0", "xh")
    in_specs = (P("ka", ja, "ia"), P("ka", "ia"), P("ia", ja), P("ia", "ka"))
    return jax.shard_map(
        local, mesh=fine, in_specs=in_specs, out_specs=P("ka", "ia"), check_vma=False
    )
```

```python
import functools

import jax
import jax.numpy as jnp
from jax import lax
from jax.experimental import pallas as pl
from jax.experimental.pallas import tpu as pltpu
from jax.sharding import Mesh, PartitionSpec as P

ORDER = [13, 0, 1, 2, 3, 4, 5, 6, 7, 8, 9, 10, 11, 12, 14, 15]
XAX, YAX = ("y0", "xh", "ka"), ("y2", "y1", "y0")
XORD = [2, 0, 1, 3, 4, 5, 6, 7]
YORD = [4, 0, 1, 2, 3, 5, 6, 7]
EARLY, GROUP = 13, 3
VMEM, HBM = pl.BlockSpec(memory_space=pltpu.VMEM), pl.BlockSpec(memory_space=pltpu.HBM)
HIGHEST = lax.Precision.HIGHEST
BF16, F32 = jnp.bfloat16, jnp.float32


def in_hbm(array):
    return pltpu.with_memory_space_constraint(array, pltpu.HBM)


def dot(x, y, precision=None):
    return jnp.dot(x, y, preferred_element_type=F32, precision=precision)


def halves_of(value):
    high = value.astype(BF16)
    return high, (value - high.astype(F32)).astype(BF16)


def message_kernel(b_ref, c_ref, out_ref):
    peers, _, size = out_ref.shape
    share, rows_j = b_ref.shape
    planes = c_ref.shape[1]
    parts = [b_ref[r : r + 1, :] for r in range(share)]
    parts += [c_ref[r : r + 1, :] for r in range(share)]
    pad = size - share * (rows_j + planes)
    if pad:
        parts.append(jnp.zeros((1, pad), F32))
    line = jnp.concatenate(parts, axis=1)
    out_ref[...] = jnp.broadcast_to(line[None], (peers, 1, size))


def split_kernel(t_ref, hi_ref, lo_ref, stage, sems):
    planes, rows_j, _ = stage.shape
    copies = [pltpu.make_async_copy(t_ref.at[k], stage.at[k], sems.at[k]) for k in range(planes)]
    for copy in copies:
        copy.start()
    for k, copy in enumerate(copies):
        copy.wait()
        rows = pl.ds(k * rows_j, rows_j)
        hi_ref[rows, :], lo_ref[rows, :] = halves_of(stage[k])


def product_kernel(got_ref, t_ref, *refs, share, early):
    if early:
        hi_ref, lo_ref, *refs = refs
    acc_ref, gram_ref, b_ref, c_ref, w_ref, stage, sems = refs
    rows_j, cols = b_ref.shape[1], t_ref.shape[2]
    planes = t_ref.shape[0]
    ranks = b_ref.shape[0]

    def copy_of(k):
        return pltpu.make_async_copy(t_ref.at[early + k], stage.at[k], sems.at[k])

    for k in range(planes - early):
        copy_of(k).start()

    @pl.when(lax.axis_index("ka") < 2)
    def _():
        for place, ia in enumerate(ORDER):
            line = got_ref[place, 0:1, :]
            for r in range(share):
                row = ia * share + r
                b_ref[row : row + 1, :] = line[:, r * rows_j : (r + 1) * rows_j]
                first = share * rows_j + r * planes
                c_ref[row : row + 1, :] = line[:, first : first + planes]
        b, c = b_ref[...], c_ref[...]
        gram_ref[...] = dot(b, b.T, HIGHEST) * dot(c, c.T, HIGHEST)
        low = jnp.zeros((ranks, cols), F32)
        total = jnp.zeros((2 * ranks, cols), F32)
        for k in range(planes):
            w_hi, w_lo = halves_of(b * c[:, k : k + 1])
            both = jnp.concatenate([w_hi, w_lo])
            if k < early:
                rows = pl.ds(k * rows_j, rows_j)
                total += dot(both, hi_ref[rows, :])
                low += dot(w_hi, lo_ref[rows, :])
            else:
                w_ref[:, pl.ds((k - early) * rows_j, rows_j)] = both
        acc_ref[...] = total[:ranks] + total[ranks:] + low

    def step(g, carry):
        for k in range(GROUP):
            copy_of(g * GROUP + k).wait()
        total = jnp.zeros((2 * ranks, cols), F32)
        low = acc_ref[...]
        for k in range(GROUP):
            at = g * GROUP + k
            t_hi, t_lo = halves_of(stage[at])
            both = w_ref[:, pl.ds(pl.multiple_of(at * rows_j, rows_j), rows_j)]
            total += dot(both, t_hi)
            low += dot(both[:ranks], t_lo)
        acc_ref[...] = total[:ranks] + total[ranks:] + low
        return carry

    lax.fori_loop(0, (planes - early) // GROUP, step, 0)


def subtract_kernel(sum_ref, gram_ref, own_ref, other_ref, out_ref):
    first_a = lax.axis_index("ka") == 0
    own, other = own_ref[...], other_ref[...]
    all_a = jnp.concatenate([jnp.where(first_a, own, other), jnp.where(first_a, other, own)])
    value = sum_ref[...] - dot(gram_ref[...], all_a, HIGHEST)
    part = out_ref.shape[1]
    for place, m in enumerate(XORD):
        at = (2 * (m % 2) + m // 4) * part
        out_ref[place] = value[at : at + part]


def size_of(axes):
    size = 1
    for axis in axes:
        size *= lax.axis_size(axis)
    return size


def local(tensor, factor_a, factor_b, factor_c):
    planes, rows_j, cols = tensor.shape
    share = factor_b.shape[0]
    half = factor_a.shape[0]
    peers = lax.axis_size("ia")
    ranks = peers * share
    size = -(-share * (rows_j + planes) // 128) * 128
    message = pl.pallas_call(
        message_kernel,
        out_shape=jax.ShapeDtypeStruct((peers, 1, size), F32),
        in_specs=[VMEM, VMEM],
        out_specs=VMEM,
        compiler_params=pltpu.CompilerParams(vmem_limit_bytes=2**20),
    )(in_hbm(factor_b), in_hbm(factor_c))
    got = lax.all_to_all(message, "ia", 0, 0, tiled=True, axis_index_groups=[ORDER])
    other = lax.ppermute(factor_a, "ka", [(0, 1), (1, 0)])
    tensor = in_hbm(tensor)
    early = []
    if EARLY:
        depth = EARLY * rows_j
        early = pl.pallas_call(
            split_kernel,
            out_shape=[pltpu.VMEM((depth, cols), BF16)] * 2,
            in_specs=[HBM],
            out_specs=[VMEM, VMEM],
            scratch_shapes=[pltpu.VMEM((EARLY, rows_j, cols), F32), pltpu.SemaphoreType.DMA((EARLY,))],
            cost_estimate=pl.CostEstimate(
                flops=4 * depth * cols, bytes_accessed=8 * depth * cols, transcendentals=0
            ),
            compiler_params=pltpu.CompilerParams(vmem_limit_bytes=8 * 2**20),
        )(tensor)
    late = planes - EARLY
    wide_x = size_of(XAX)
    partial, gram = pl.pallas_call(
        functools.partial(product_kernel, share=share, early=EARLY),
        out_shape=[jax.ShapeDtypeStruct((ranks, cols), F32), jax.ShapeDtypeStruct((ranks, ranks), F32)],
        in_specs=[VMEM, HBM] + [VMEM] * len(early),
        out_specs=[VMEM, VMEM],
        scratch_shapes=[
            pltpu.VMEM((ranks, rows_j), F32),
            pltpu.VMEM((ranks, planes), F32),
            pltpu.VMEM((2 * ranks, late * rows_j), BF16),
            pltpu.VMEM((late, rows_j, cols), F32),
            pltpu.SemaphoreType.DMA((late,)),
        ],
        cost_estimate=pl.CostEstimate(
            flops=6 * ranks * planes * rows_j * cols,
            bytes_accessed=4 * planes * rows_j * cols,
            transcendentals=0,
        ),
        compiler_params=pltpu.CompilerParams(vmem_limit_bytes=12 * 2**20),
    )(got, tensor, *early)
    mine = pl.pallas_call(
        subtract_kernel,
        out_shape=jax.ShapeDtypeStruct((wide_x, half // 2, cols), F32),
        in_specs=[VMEM] * 4,
        out_specs=VMEM,
        compiler_params=pltpu.CompilerParams(vmem_limit_bytes=2 * 2**20),
    )(partial, gram, factor_a, other)
    x_sum = jnp.sum(lax.all_to_all(mine, XAX, 0, 0, tiled=True, axis_index_groups=[XORD]), 0)
    wide_y = size_of(YAX)
    y_parts = lax.all_to_all(
        jnp.broadcast_to(x_sum[None], (wide_y, half // 2, cols)), YAX, 0, 0, tiled=True, axis_index_groups=[YORD]
    )
    sides = []
    for side in range(2):
        sides.append(sum(y_parts[place] for place, m in enumerate(YORD) if m % 2 == side))
    return jnp.concatenate(sides)


def solution(mesh):
    sizes = mesh.devices.shape
    fine = Mesh(
        mesh.devices.reshape(sizes[0], sizes[1] // 8, 2, 2, 2, sizes[2]),
        ("ia", "y2", "y1", "y0", "xh", "ka"),
    )
    ja = ("y2", "y1", "y0", "xh")
    in_specs = (P("ka", ja, "ia"), P("ka", "ia"), P("ia", ja), P("ia", "ka"))
    return jax.shard_map(
        local, mesh=fine, in_specs=in_specs, out_specs=P("ka", "ia"), check_vma=False
    )
```

```python
import functools

import jax
import jax.numpy as jnp
from jax import lax
from jax.experimental import pallas as pl
from jax.experimental.pallas import tpu as pltpu
from jax.sharding import Mesh, PartitionSpec as P

ORDER = [13, 0, 1, 2, 3, 4, 5, 6, 7, 8, 9, 10, 11, 12, 14, 15]
XAX, YAX = ("y0", "xh", "ka"), ("y2", "y1", "y0")
XORD = [2, 0, 1, 3, 4, 5, 6, 7]
YORD = [4, 0, 1, 2, 3, 5, 6, 7]
EARLY, GROUP = 13, 3
FIRST = 6
VMEM, HBM = pl.BlockSpec(memory_space=pltpu.VMEM), pl.BlockSpec(memory_space=pltpu.HBM)
ANY = pl.BlockSpec(memory_space=pl.ANY)
HIGHEST = lax.Precision.HIGHEST
BF16, F32 = jnp.bfloat16, jnp.float32


def in_hbm(array):
    return pltpu.with_memory_space_constraint(array, pltpu.HBM)


def dot(x, y, precision=None):
    return jnp.dot(x, y, preferred_element_type=F32, precision=precision)


def halves_of(value):
    high = value.astype(BF16)
    return high, (value - high.astype(F32)).astype(BF16)


def message_kernel(b_ref, c_ref, t_ref, out_ref, hi_ref, lo_ref, stage, sems):
    peers, _, size = out_ref.shape
    share, rows_j = b_ref.shape
    planes = c_ref.shape[1]
    parts = [b_ref[r : r + 1, :] for r in range(share)]
    parts += [c_ref[r : r + 1, :] for r in range(share)]
    pad = size - share * (rows_j + planes)
    if pad:
        parts.append(jnp.zeros((1, pad), F32))
    line = jnp.concatenate(parts, axis=1)
    out_ref[...] = jnp.broadcast_to(line[None], (peers, 1, size))

    @pl.when(lax.axis_index("ia") < FIRST)
    def _():
        split(t_ref, hi_ref, lo_ref, stage, sems)


def split(t_ref, hi_ref, lo_ref, stage, sems):
    planes, rows_j, _ = stage.shape
    copies = [pltpu.make_async_copy(t_ref.at[k], stage.at[k], sems.at[k]) for k in range(planes)]
    for copy in copies:
        copy.start()
    for k, copy in enumerate(copies):
        copy.wait()
        rows = pl.ds(k * rows_j, rows_j)
        hi_ref[rows, :], lo_ref[rows, :] = halves_of(stage[k])


def split_kernel(t_ref, hi_in, lo_in, hi_ref, lo_ref, hi, lo, stage, sems, out_sems):
    del hi_in, lo_in

    @pl.when(lax.axis_index("ia") >= FIRST)
    def _():
        split(t_ref, hi, lo, stage, sems)
        copies = [
            pltpu.make_async_copy(hi, hi_ref, out_sems.at[0]),
            pltpu.make_async_copy(lo, lo_ref, out_sems.at[1]),
        ]
        for copy in copies:
            copy.start()
        for copy in copies:
            copy.wait()


def product_kernel(got_ref, t_ref, *refs, share, early):
    if early:
        hi_ref, lo_ref, *refs = refs
    acc_ref, gram_ref, b_ref, c_ref, w_ref, stage, sems = refs
    rows_j, cols = b_ref.shape[1], t_ref.shape[2]
    planes = t_ref.shape[0]
    ranks = b_ref.shape[0]

    def copy_of(k):
        return pltpu.make_async_copy(t_ref.at[early + k], stage.at[k], sems.at[k])

    for k in range(planes - early):
        copy_of(k).start()

    @pl.when(lax.axis_index("ka") < 2)
    def _():
        for place, ia in enumerate(ORDER):
            line = got_ref[place, 0:1, :]
            for r in range(share):
                row = ia * share + r
                b_ref[row : row + 1, :] = line[:, r * rows_j : (r + 1) * rows_j]
                first = share * rows_j + r * planes
                c_ref[row : row + 1, :] = line[:, first : first + planes]
        b, c = b_ref[...], c_ref[...]
        gram_ref[...] = dot(b, b.T, HIGHEST) * dot(c, c.T, HIGHEST)
        low = jnp.zeros((ranks, cols), F32)
        total = jnp.zeros((2 * ranks, cols), F32)
        for k in range(planes):
            w_hi, w_lo = halves_of(b * c[:, k : k + 1])
            both = jnp.concatenate([w_hi, w_lo])
            if k < early:
                rows = pl.ds(k * rows_j, rows_j)
                total += dot(both, hi_ref[rows, :])
                low += dot(w_hi, lo_ref[rows, :])
            else:
                w_ref[:, pl.ds((k - early) * rows_j, rows_j)] = both
        acc_ref[...] = total[:ranks] + total[ranks:] + low

    def step(g, carry):
        for k in range(GROUP):
            copy_of(g * GROUP + k).wait()
        total = jnp.zeros((2 * ranks, cols), F32)
        low = acc_ref[...]
        for k in range(GROUP):
            at = g * GROUP + k
            t_hi, t_lo = halves_of(stage[at])
            both = w_ref[:, pl.ds(pl.multiple_of(at * rows_j, rows_j), rows_j)]
            total += dot(both, t_hi)
            low += dot(both[:ranks], t_lo)
        acc_ref[...] = total[:ranks] + total[ranks:] + low
        return carry

    lax.fori_loop(0, (planes - early) // GROUP, step, 0)


def subtract_kernel(sum_ref, gram_ref, own_ref, other_ref, out_ref):
    first_a = lax.axis_index("ka") == 0
    own, other = own_ref[...], other_ref[...]
    all_a = jnp.concatenate([jnp.where(first_a, own, other), jnp.where(first_a, other, own)])
    value = sum_ref[...] - dot(gram_ref[...], all_a, HIGHEST)
    part = out_ref.shape[1]
    for place, m in enumerate(XORD):
        at = (2 * (m % 2) + m // 4) * part
        out_ref[place] = value[at : at + part]


def size_of(axes):
    size = 1
    for axis in axes:
        size *= lax.axis_size(axis)
    return size


def local(tensor, factor_a, factor_b, factor_c):
    planes, rows_j, cols = tensor.shape
    share = factor_b.shape[0]
    half = factor_a.shape[0]
    peers = lax.axis_size("ia")
    ranks = peers * share
    size = -(-share * (rows_j + planes) // 128) * 128
    tensor = in_hbm(tensor)
    depth = EARLY * rows_j
    stage = [pltpu.VMEM((EARLY, rows_j, cols), F32), pltpu.SemaphoreType.DMA((EARLY,))]
    halves = pltpu.VMEM((depth, cols), BF16)
    message, *early = pl.pallas_call(
        message_kernel,
        out_shape=[jax.ShapeDtypeStruct((peers, 1, size), F32), halves, halves],
        in_specs=[VMEM, VMEM, HBM],
        out_specs=[VMEM] * 3,
        scratch_shapes=stage,
        compiler_params=pltpu.CompilerParams(vmem_limit_bytes=9 * 2**20),
    )(in_hbm(factor_b), in_hbm(factor_c), tensor)
    got = lax.all_to_all(message, "ia", 0, 0, tiled=True, axis_index_groups=[ORDER])
    other = lax.ppermute(factor_a, "ka", [(0, 1), (1, 0)])
    early = pl.pallas_call(
        split_kernel,
        out_shape=[halves, halves],
        in_specs=[HBM, ANY, ANY],
        out_specs=[ANY, ANY],
        scratch_shapes=[halves, halves] + stage + [pltpu.SemaphoreType.DMA((2,))],
        input_output_aliases={1: 0, 2: 1},
        cost_estimate=pl.CostEstimate(
            flops=4 * depth * cols, bytes_accessed=8 * depth * cols, transcendentals=0
        ),
        compiler_params=pltpu.CompilerParams(vmem_limit_bytes=9 * 2**20),
    )(tensor, *early)
    late = planes - EARLY
    wide_x = size_of(XAX)
    partial, gram = pl.pallas_call(
        functools.partial(product_kernel, share=share, early=EARLY),
        out_shape=[jax.ShapeDtypeStruct((ranks, cols), F32), jax.ShapeDtypeStruct((ranks, ranks), F32)],
        in_specs=[VMEM, HBM] + [VMEM] * len(early),
        out_specs=[VMEM, VMEM],
        scratch_shapes=[
            pltpu.VMEM((ranks, rows_j), F32),
            pltpu.VMEM((ranks, planes), F32),
            pltpu.VMEM((2 * ranks, late * rows_j), BF16),
            pltpu.VMEM((late, rows_j, cols), F32),
            pltpu.SemaphoreType.DMA((late,)),
        ],
        cost_estimate=pl.CostEstimate(
            flops=6 * ranks * planes * rows_j * cols,
            bytes_accessed=4 * planes * rows_j * cols,
            transcendentals=0,
        ),
        compiler_params=pltpu.CompilerParams(vmem_limit_bytes=12 * 2**20),
    )(got, tensor, *early)
    mine = pl.pallas_call(
        subtract_kernel,
        out_shape=jax.ShapeDtypeStruct((wide_x, half // 2, cols), F32),
        in_specs=[VMEM] * 4,
        out_specs=VMEM,
        compiler_params=pltpu.CompilerParams(vmem_limit_bytes=2 * 2**20),
    )(partial, gram, factor_a, other)
    x_sum = jnp.sum(lax.all_to_all(mine, XAX, 0, 0, tiled=True, axis_index_groups=[XORD]), 0)
    wide_y = size_of(YAX)
    y_parts = lax.all_to_all(
        jnp.broadcast_to(x_sum[None], (wide_y, half // 2, cols)), YAX, 0, 0, tiled=True, axis_index_groups=[YORD]
    )
    sides = []
    for side in range(2):
        sides.append(sum(y_parts[place] for place, m in enumerate(YORD) if m % 2 == side))
    return jnp.concatenate(sides)


def solution(mesh):
    sizes = mesh.devices.shape
    fine = Mesh(
        mesh.devices.reshape(sizes[0], sizes[1] // 8, 2, 2, 2, sizes[2]),
        ("ia", "y2", "y1", "y0", "xh", "ka"),
    )
    ja = ("y2", "y1", "y0", "xh")
    in_specs = (P("ka", ja, "ia"), P("ka", "ia"), P("ia", ja), P("ia", "ka"))
    return jax.shard_map(
        local, mesh=fine, in_specs=in_specs, out_specs=P("ka", "ia"), check_vma=False
    )
```

```python
import functools

import jax
import jax.numpy as jnp
from jax import lax
from jax.experimental import pallas as pl
from jax.experimental.pallas import tpu as pltpu
from jax.sharding import Mesh, PartitionSpec as P

ORDER = [13, 0, 1, 2, 3, 4, 5, 6, 7, 8, 9, 10, 11, 12, 14, 15]
XAX, YAX = ("y0", "xh", "ka"), ("y2", "y1", "y0")
XORD = [2, 0, 1, 3, 4, 5, 6, 7]
YORD = [4, 0, 1, 2, 3, 5, 6, 7]
EARLY, GROUP = 13, 3
FIRST = 6
VMEM, HBM = pl.BlockSpec(memory_space=pltpu.VMEM), pl.BlockSpec(memory_space=pltpu.HBM)
ANY = pl.BlockSpec(memory_space=pl.ANY)
HIGHEST = lax.Precision.HIGHEST
BF16, F32 = jnp.bfloat16, jnp.float32


def in_hbm(array):
    return pltpu.with_memory_space_constraint(array, pltpu.HBM)


def dot(x, y, precision=None):
    return jnp.dot(x, y, preferred_element_type=F32, precision=precision)


def halves_of(value):
    high = value.astype(BF16)
    return high, (value - high.astype(F32)).astype(BF16)


def message_kernel(b_ref, c_ref, out_ref):
    peers, _, size = out_ref.shape
    share, rows_j = b_ref.shape
    planes = c_ref.shape[1]
    parts = [b_ref[r : r + 1, :] for r in range(share)]
    parts += [c_ref[r : r + 1, :] for r in range(share)]
    pad = size - share * (rows_j + planes)
    if pad:
        parts.append(jnp.zeros((1, pad), F32))
    line = jnp.concatenate(parts, axis=1)
    out_ref[...] = jnp.broadcast_to(line[None], (peers, 1, size))


def early_kernel(t_ref, hi_ref, lo_ref, stage, sems):
    @pl.when(lax.axis_index("ia") < FIRST)
    def _():
        split(t_ref, hi_ref, lo_ref, stage, sems)


def split(t_ref, hi_ref, lo_ref, stage, sems):
    planes, rows_j, _ = stage.shape
    copies = [pltpu.make_async_copy(t_ref.at[k], stage.at[k], sems.at[k]) for k in range(planes)]
    for copy in copies:
        copy.start()
    for k, copy in enumerate(copies):
        copy.wait()
        rows = pl.ds(k * rows_j, rows_j)
        hi_ref[rows, :], lo_ref[rows, :] = halves_of(stage[k])


def split_kernel(t_ref, hi_in, lo_in, hi_ref, lo_ref, hi, lo, stage, sems, out_sems):
    del hi_in, lo_in

    @pl.when(lax.axis_index("ia") >= FIRST)
    def _():
        split(t_ref, hi, lo, stage, sems)
        copies = [
            pltpu.make_async_copy(hi, hi_ref, out_sems.at[0]),
            pltpu.make_async_copy(lo, lo_ref, out_sems.at[1]),
        ]
        for copy in copies:
            copy.start()
        for copy in copies:
            copy.wait()


def product_kernel(got_ref, t_ref, *refs, share, early):
    if early:
        hi_ref, lo_ref, *refs = refs
    acc_ref, gram_ref, b_ref, c_ref, w_ref, stage, sems = refs
    rows_j, cols = b_ref.shape[1], t_ref.shape[2]
    planes = t_ref.shape[0]
    ranks = b_ref.shape[0]

    def copy_of(k):
        return pltpu.make_async_copy(t_ref.at[early + k], stage.at[k], sems.at[k])

    for k in range(planes - early):
        copy_of(k).start()

    @pl.when(lax.axis_index("ka") < 2)
    def _():
        for place, ia in enumerate(ORDER):
            line = got_ref[place, 0:1, :]
            for r in range(share):
                row = ia * share + r
                b_ref[row : row + 1, :] = line[:, r * rows_j : (r + 1) * rows_j]
                first = share * rows_j + r * planes
                c_ref[row : row + 1, :] = line[:, first : first + planes]
        b, c = b_ref[...], c_ref[...]
        gram_ref[...] = dot(b, b.T, HIGHEST) * dot(c, c.T, HIGHEST)
        low = jnp.zeros((ranks, cols), F32)
        total = jnp.zeros((2 * ranks, cols), F32)
        for k in range(planes):
            w_hi, w_lo = halves_of(b * c[:, k : k + 1])
            both = jnp.concatenate([w_hi, w_lo])
            if k < early:
                rows = pl.ds(k * rows_j, rows_j)
                total += dot(both, hi_ref[rows, :])
                low += dot(w_hi, lo_ref[rows, :])
            else:
                w_ref[:, pl.ds((k - early) * rows_j, rows_j)] = both
        acc_ref[...] = total[:ranks] + total[ranks:] + low

    def step(g, carry):
        for k in range(GROUP):
            copy_of(g * GROUP + k).wait()
        total = jnp.zeros((2 * ranks, cols), F32)
        low = acc_ref[...]
        for k in range(GROUP):
            at = g * GROUP + k
            t_hi, t_lo = halves_of(stage[at])
            both = w_ref[:, pl.ds(pl.multiple_of(at * rows_j, rows_j), rows_j)]
            total += dot(both, t_hi)
            low += dot(both[:ranks], t_lo)
        acc_ref[...] = total[:ranks] + total[ranks:] + low
        return carry

    lax.fori_loop(0, (planes - early) // GROUP, step, 0)


def subtract_kernel(sum_ref, gram_ref, own_ref, other_ref, out_ref):
    first_a = lax.axis_index("ka") == 0
    own, other = own_ref[...], other_ref[...]
    all_a = jnp.concatenate([jnp.where(first_a, own, other), jnp.where(first_a, other, own)])
    value = sum_ref[...] - dot(gram_ref[...], all_a, HIGHEST)
    part = out_ref.shape[1]
    for place, m in enumerate(XORD):
        at = (2 * (m % 2) + m // 4) * part
        out_ref[place] = value[at : at + part]


def size_of(axes):
    size = 1
    for axis in axes:
        size *= lax.axis_size(axis)
    return size


def local(tensor, factor_a, factor_b, factor_c):
    planes, rows_j, cols = tensor.shape
    share = factor_b.shape[0]
    half = factor_a.shape[0]
    peers = lax.axis_size("ia")
    ranks = peers * share
    size = -(-share * (rows_j + planes) // 128) * 128
    tensor = in_hbm(tensor)
    depth = EARLY * rows_j
    stage = [pltpu.VMEM((EARLY, rows_j, cols), F32), pltpu.SemaphoreType.DMA((EARLY,))]
    halves = pltpu.VMEM((depth, cols), BF16)
    early = pl.pallas_call(
        early_kernel,
        out_shape=[halves, halves],
        in_specs=[HBM],
        out_specs=[VMEM] * 2,
        scratch_shapes=stage,
        compiler_params=pltpu.CompilerParams(vmem_limit_bytes=9 * 2**20),
    )(tensor)
    factor_b, factor_c, *early = lax.optimization_barrier((factor_b, factor_c, *early))
    message = pl.pallas_call(
        message_kernel,
        out_shape=jax.ShapeDtypeStruct((peers, 1, size), F32),
        in_specs=[VMEM] * 2,
        out_specs=VMEM,
        compiler_params=pltpu.CompilerParams(vmem_limit_bytes=2**20),
    )(factor_b, factor_c)
    got = lax.all_to_all(message, "ia", 0, 0, tiled=True, axis_index_groups=[ORDER])
    other = lax.ppermute(factor_a, "ka", [(0, 1), (1, 0)])
    early = pl.pallas_call(
        split_kernel,
        out_shape=[halves, halves],
        in_specs=[HBM, ANY, ANY],
        out_specs=[ANY, ANY],
        scratch_shapes=[halves, halves] + stage + [pltpu.SemaphoreType.DMA((2,))],
        input_output_aliases={1: 0, 2: 1},
        cost_estimate=pl.CostEstimate(
            flops=4 * depth * cols, bytes_accessed=8 * depth * cols, transcendentals=0
        ),
        compiler_params=pltpu.CompilerParams(vmem_limit_bytes=9 * 2**20),
    )(tensor, *early)
    late = planes - EARLY
    wide_x = size_of(XAX)
    partial, gram = pl.pallas_call(
        functools.partial(product_kernel, share=share, early=EARLY),
        out_shape=[jax.ShapeDtypeStruct((ranks, cols), F32), jax.ShapeDtypeStruct((ranks, ranks), F32)],
        in_specs=[VMEM, HBM] + [VMEM] * len(early),
        out_specs=[VMEM, VMEM],
        scratch_shapes=[
            pltpu.VMEM((ranks, rows_j), F32),
            pltpu.VMEM((ranks, planes), F32),
            pltpu.VMEM((2 * ranks, late * rows_j), BF16),
            pltpu.VMEM((late, rows_j, cols), F32),
            pltpu.SemaphoreType.DMA((late,)),
        ],
        cost_estimate=pl.CostEstimate(
            flops=6 * ranks * planes * rows_j * cols,
            bytes_accessed=4 * planes * rows_j * cols,
            transcendentals=0,
        ),
        compiler_params=pltpu.CompilerParams(vmem_limit_bytes=12 * 2**20),
    )(got, tensor, *early)
    mine = pl.pallas_call(
        subtract_kernel,
        out_shape=jax.ShapeDtypeStruct((wide_x, half // 2, cols), F32),
        in_specs=[VMEM] * 4,
        out_specs=VMEM,
        compiler_params=pltpu.CompilerParams(vmem_limit_bytes=2 * 2**20),
    )(partial, gram, factor_a, other)
    x_sum = jnp.sum(lax.all_to_all(mine, XAX, 0, 0, tiled=True, axis_index_groups=[XORD]), 0)
    wide_y = size_of(YAX)
    y_parts = lax.all_to_all(
        jnp.broadcast_to(x_sum[None], (wide_y, half // 2, cols)), YAX, 0, 0, tiled=True, axis_index_groups=[YORD]
    )
    sides = []
    for side in range(2):
        sides.append(sum(y_parts[place] for place, m in enumerate(YORD) if m % 2 == side))
    return jnp.concatenate(sides)


def solution(mesh):
    sizes = mesh.devices.shape
    fine = Mesh(
        mesh.devices.reshape(sizes[0], sizes[1] // 8, 2, 2, 2, sizes[2]),
        ("ia", "y2", "y1", "y0", "xh", "ka"),
    )
    ja = ("y2", "y1", "y0", "xh")
    in_specs = (P("ka", ja, "ia"), P("ka", "ia"), P("ia", ja), P("ia", "ka"))
    return jax.shard_map(
        local, mesh=fine, in_specs=in_specs, out_specs=P("ka", "ia"), check_vma=False
    )
```
